32 devices in a mesh: row: 4 (over z), col: 4 (over y, core), depth: 2 (over x).
Axes of the slice: x: 2, y: 2, z: 4, core: 2. Of those that a mesh axis runs over, the one named last changes fastest.
Arguments:
- tokens: bfloat16 [768, 12288], P(('col', 'depth'), 'row'), may hold values from -6 to 6
- w_up: bfloat16 [12288, 24576], P(('row', 'depth'), 'col'), may hold values from -0.0546875 to 0.0546875
- w_down: bfloat16 [24576, 12288], P('col', ('row', 'depth')), may hold values from -0.0390625 to 0.0390625
- cotangent: bfloat16 [768, 12288], P(('col', 'depth'), 'row'), may hold values from -6 to 6
Outputs:
- output: bfloat16 [768, 12288], P(('col', 'depth'), 'row')
- grad_tokens: bfloat16 [768, 12288], P(('col', 'depth'), 'row')
- grad_up: bfloat16 [12288, 24576], P(('row', 'depth'), 'col')
- grad_down: bfloat16 [24576, 12288], P('col', ('row', 'depth'))
The draws below stay inside these ranges and needn't reach their ends.
All inputs are finite; a program needn't handle non-finite values.
Results may differ from the reference program's by a relative error of at most 0.0059.
Values may be sent and summed in bfloat16 or wider, within the bound.
A program may use at most 384 MiB of HBM per device.

```python
import math
import jax
import jax.numpy as jnp
from jax import lax

D = 12288
FF = 24576
TOK_GROUP = 384
TOKENS = 768
N_COL = 4
N_DEPTH = 2


def block_scale(rng, dims, cuts, low, high):
    gain = 1.0
    for dim, blocks in cuts:
        steps = jax.random.uniform(jax.random.fold_in(jax.random.fold_in(rng, 6), dim), (blocks,), jnp.float32, low / len(cuts), high / len(cuts))
        gain = gain * jnp.repeat(jnp.exp(steps), dims[dim] // blocks).reshape((-1,) + (1,) * (len(dims) - 1 - dim))
    return gain


def noise(stream_key, shape, deviation, bound, pieces=(), kind=jnp.bfloat16):
    values = jax.random.normal(stream_key, shape, jnp.float32) * deviation
    if len(pieces) > 0:
        values = block_scale(stream_key, shape, pieces, -0.22, 0.18) * values
    return jnp.clip(values, min=-bound, max=bound).astype(kind)


def setup_inputs(seed: int = 0) -> dict:
    key_of = jax.random.split(jax.random.key(seed), 5)
    return {
        "tokens": noise(key_of[0], (TOKENS, D), 1.0, 6.0, ((0, 8), (1, 4))),
        "w_up": noise(key_of[1], (D, FF), D ** -0.5, 0.0546875, ((0, 8), (1, 4))),
        "w_down": noise(key_of[2], (FF, D), FF ** -0.5, 0.0390625, ((0, 4), (1, 8))),
        "cotangent": noise(key_of[3], (TOKENS, D), 1.0, 6.0, ((0, 8), (1, 4))),
    }


root_coeff = math.sqrt(2.0 / math.pi)

def gelu_pair(pre_act):
    inner_arg = root_coeff * (pre_act + 0.044715 * pre_act * pre_act * pre_act)
    tangent = jnp.tanh(inner_arg)
    gelu_value = 0.5 * pre_act * (1.0 + tangent)
    gelu_slope = 0.5 * (1.0 + tangent) + 0.5 * pre_act * (1.0 - tangent * tangent) * root_coeff * (1.0 + 0.134145 * pre_act * pre_act)
    return (gelu_value, gelu_slope)

def depth_grad(left_side, right_side):
    block = TOK_GROUP // N_COL
    left_parts = left_side.reshape(N_COL, N_DEPTH, block, left_side.shape[1])
    right_parts = right_side.reshape(N_COL, N_DEPTH, block, right_side.shape[1])
    accum = jnp.zeros((left_side.shape[1], right_side.shape[1]), jnp.float32)
    for index_depth in range(N_DEPTH):
        left_rows = left_parts[:, index_depth].reshape(-1, left_side.shape[1])
        right_rows = right_parts[:, index_depth].reshape(-1, right_side.shape[1])
        partial_grad = jnp.dot(left_rows.T, right_rows, preferred_element_type=jnp.float32)
        accum = accum + lax.optimization_barrier(partial_grad.astype(jnp.bfloat16)).astype(jnp.float32)
    return accum.astype(jnp.bfloat16)

def reference(tokens, w_up, w_down, cotangent):
    pre_act = jnp.dot(tokens, w_up, preferred_element_type=jnp.float32)
    gelu_value, gelu_slope = gelu_pair(pre_act)
    hidden = gelu_value.astype(jnp.bfloat16)
    output = jnp.dot(hidden, w_down, preferred_element_type=jnp.float32).astype(jnp.bfloat16)
    d_hidden = jnp.dot(cotangent, w_down.T, preferred_element_type=jnp.float32)
    d_pre = (d_hidden * gelu_slope).astype(jnp.bfloat16)
    grad_tokens = jnp.dot(d_pre, w_up.T, preferred_element_type=jnp.float32).astype(jnp.bfloat16)
    grad_up = depth_grad(tokens, d_pre)
    grad_down = depth_grad(hidden, cotangent)
    return (output, grad_tokens, grad_up, grad_down)
```

```python
import math

import jax
import jax.numpy as jnp
from jax import lax
from jax.sharding import PartitionSpec as P

root_coeff = math.sqrt(2.0 / math.pi)
CHUNKS = 6
LEAD = 2


def gelu_pair(pre_act):
    inner_arg = root_coeff * (pre_act + 0.044715 * pre_act * pre_act * pre_act)
    tangent = jnp.tanh(inner_arg)
    gelu_value = 0.5 * pre_act * (1.0 + tangent)
    gelu_slope = 0.5 * (1.0 + tangent) + 0.5 * pre_act * (1.0 - tangent * tangent) * root_coeff * (
        1.0 + 0.134145 * pre_act * pre_act
    )
    return (gelu_value, gelu_slope)


def swap(value, axis, mask):
    size = lax.axis_size(axis)
    return lax.ppermute(value, axis, [(i, i ^ mask) for i in range(size)])


def reorder(rows, count, mask):
    height = rows.shape[0] // count
    pieces = [lax.dynamic_slice_in_dim(rows, (i ^ mask) * height, height, 0) for i in range(count)]
    return jnp.concatenate(pieces, axis=0)


def dot_rows(left, right):
    return jnp.dot(left, right, preferred_element_type=jnp.float32)


def dot_rows_t(left, right):
    return lax.dot_general(left, right, (((1,), (1,)), ((), ())), preferred_element_type=jnp.float32)


def dot_tokens(left, right):
    return lax.dot_general(left, right, (((0,), (0,)), ((), ())), preferred_element_type=jnp.float32)


def half(value):
    return value.astype(jnp.bfloat16)


def bits_of(size):
    return [1 << b for b in range(size.bit_length() - 1)]


def gather_tokens(local, depth_at, n_depth, n_cols):
    block = local.shape[0]
    width = local.shape[1] // n_depth
    parts = [
        lax.dynamic_slice_in_dim(local, (depth_at ^ k) * width, width, 1) for k in range(n_depth)
    ]
    parts = [parts[0]] + [swap(parts[k], "depth", k) for k in range(1, n_depth)]
    held = jnp.stack(parts)[None]
    done = 1
    for bit in reversed(bits_of(n_cols)):
        other = swap(held, "col", bit)
        held = jnp.stack([held, other], axis=1).reshape((2 * done,) + held.shape[1:])
        done *= 2
    return held.reshape(n_cols * n_depth * block, width)


def scatter_output(total, n_depth, n_cols, depth_at, beside):
    width = total.shape[1]
    beside = list(beside)
    held = total.reshape(n_cols, -1, width)
    for step, bit in enumerate(bits_of(n_cols)):
        held = held.reshape((held.shape[0] // 2, 2) + held.shape[1:])
        held = held[:, 0] + swap(half(held[:, 1]), "col", bit).astype(jnp.float32)
        if step < len(beside):
            held, beside[step] = lax.optimization_barrier((held, beside[step]))
    mine = half(held[0]).reshape(n_depth, -1, width)
    parts = [mine[0]] + [swap(mine[k], "depth", k) for k in range(1, n_depth)]
    joined = jnp.concatenate(parts, axis=1)
    pieces = [
        lax.dynamic_slice_in_dim(joined, (i ^ depth_at) * width, width, 1) for i in range(n_depth)
    ]
    return jnp.concatenate(pieces, axis=1), beside


class Lane:
    def __init__(self):
        self.ended = []

    def send(self, values, axis, masks):
        if len(self.ended) >= 2:
            values = lax.optimization_barrier((values, self.ended[-2]))[0]
        got = [swap(value, axis, mask) for value, mask in zip(values, masks)]
        self.ended.append(got)
        return got


def body(tokens, w_up, w_down, cotangent):
    depth_at = lax.axis_index("depth")
    n_depth = lax.axis_size("depth")
    n_cols = lax.axis_size("col")
    n_row = lax.axis_size("row")
    owners = n_depth * n_row
    fine = max(owners, n_cols * n_depth)
    owner_at = (depth_at * n_row + lax.axis_index("row")) * (fine // owners)
    token_at = (lax.axis_index("col") * n_depth + depth_at) * (fine // (n_cols * n_depth))
    mask = owner_at ^ token_at
    chunks = max(n for n in (2, 4, 6, 8) if w_up.shape[1] % (n * 128) == 0 and n <= CHUNKS)
    wide = w_up.shape[1] // chunks
    lead = min(LEAD, chunks)

    x_sub = reorder(gather_tokens(tokens, depth_at, n_depth, n_cols), fine, mask)
    cot_sub = reorder(gather_tokens(cotangent, depth_at, n_depth, n_cols), fine, mask)

    ups = [w_up[:, c * wide : (c + 1) * wide] for c in range(chunks)]
    downs = [w_down[c * wide : (c + 1) * wide] for c in range(chunks)]
    span = x_sub.shape[0] // n_depth
    block = span // n_row
    depth_lane, row_lane = Lane(), Lane()
    depth_masks = list(range(1, n_depth))
    row_masks = list(range(1, n_row))

    def make(unit, rows):
        kind, c = unit
        return dot_rows(rows, ups[c]) if kind == "up" else dot_rows_t(rows, downs[c])

    def left(unit):
        return x_sub if unit[0] == "up" else cot_sub

    units = [("up", c) for c in range(lead)]
    for c in range(chunks):
        units.append(("down", c))
        if c + lead < chunks:
            units.append(("up", c + lead))

    count = len(units)
    arrived, mine, column, whole, slopes = {}, {}, {}, {}, {}

    def reduce_depth(unit):
        rows = left(unit)
        away = [half(make(unit, rows[k * span : (k + 1) * span])) for k in depth_masks]
        arrived[unit] = depth_lane.send(away, "depth", depth_masks)

    def reduce_row(unit):
        total = make(unit, left(unit)[:span])
        for piece in arrived[unit]:
            total = total + piece.astype(jnp.float32)
        away = [half(total[k * block : (k + 1) * block]) for k in row_masks]
        result = total[:block]
        for piece in row_lane.send(away, "row", row_masks):
            result = result + piece.astype(jnp.float32)
        if unit[0] == "up":
            gelu_value, slopes[unit[1]] = gelu_pair(result)
            mine[unit] = half(gelu_value)
        else:
            mine[unit] = half(result * slopes[unit[1]])

    def gather_row(unit):
        own = mine[unit]
        got = row_lane.send([own] * len(row_masks), "row", row_masks)
        column[unit] = jnp.concatenate([own] + got, axis=0)

    def gather_depth(unit):
        own = column[unit]
        got = depth_lane.send([own] * len(depth_masks), "depth", depth_masks)
        whole[unit] = jnp.concatenate([own] + got, axis=0)

    for slot in range(count + 3):
        if slot < count:
            reduce_depth(units[slot])
        if 0 <= slot - 1 < count:
            reduce_row(units[slot - 1])
        if 0 <= slot - 2 < count:
            gather_row(units[slot - 2])
        if 0 <= slot - 3 < count:
            gather_depth(units[slot - 3])

    hidden = [whole[("up", c)] for c in range(chunks)]
    d_pre = [whole[("down", c)] for c in range(chunks)]

    def span_of(first, last):
        return slice(first * wide, last * wide)

    middle = chunks // 2
    out_part = dot_rows(jnp.concatenate(hidden[:middle], axis=1), w_down[span_of(0, middle)])
    out_part = out_part + dot_rows(
        jnp.concatenate(hidden[middle:], axis=1), w_down[span_of(middle, chunks)]
    )
    output, _ = scatter_output(reorder(out_part, fine, mask), n_depth, n_cols, depth_at, [])

    dx_part = dot_rows_t(jnp.concatenate(d_pre[:middle], axis=1), w_up[:, span_of(0, middle)])
    dx_part = dx_part + dot_rows_t(
        jnp.concatenate(d_pre[middle:-1], axis=1), w_up[:, span_of(middle, chunks - 1)]
    )
    d_pre[-1], dx_part = lax.optimization_barrier((d_pre[-1], dx_part))
    dx_part = dx_part + dot_rows_t(d_pre[-1], ups[-1])
    ordered = reorder(dx_part, fine, mask)
    hidden_all = jnp.concatenate(hidden, axis=1)
    d_pre_all = jnp.concatenate(d_pre, axis=1)
    ordered, d_pre_all, hidden_all = lax.optimization_barrier((ordered, d_pre_all, hidden_all))
    grad_up = half(dot_tokens(x_sub, d_pre_all))
    grad_down = half(dot_tokens(hidden_all, cot_sub))
    grad_tokens, (grad_up, grad_down) = scatter_output(
        ordered, n_depth, n_cols, depth_at, [grad_up, grad_down]
    )
    return (output, grad_tokens, grad_up, grad_down)


def solution(mesh):
    placed = (
        P(("col", "depth"), "row"),
        P(("row", "depth"), "col"),
        P("col", ("row", "depth")),
        P(("col", "depth"), "row"),
    )
    return jax.shard_map(
        body,
        mesh=mesh,
        in_specs=placed,
        out_specs=(
            P(("col", "depth"), "row"),
            P(("col", "depth"), "row"),
            P(("row", "depth"), "col"),
            P("col", ("row", "depth")),
        ),
        check_vma=False,
    )
```
